32 devices in a mesh: freq: 2 (over y), src: 4 (over z), rcv: 4 (over x, core).
Axes of the slice: x: 2, y: 2, z: 4, core: 2. Of those that a mesh axis runs over, the one named last changes fastest.
Arguments:
- wavefield: bfloat16 [2, 12288, 6144], P(None, ('freq', 'src'), 'rcv'), parts along dimension 1, may hold values from -2 to 2
- unrecorded: int32 [8, 4], P(('freq', 'src'), 'rcv'), parts along dimension 0, may hold values from 0 to 1, as said below
- obliquity: int32 [8, 4], P(('freq', 'src'), 'rcv'), parts along dimension 0, may hold values from 0 to 7
- scale_table: float32 [8], replicated, may hold values from 0.4 to 2.5
- panel_index: int32 [4], P('freq'), parts along dimension 0, may hold values from 0 to 7
Outputs:
- primaries: bfloat16 [2, 12288, 6144], P(None, ('freq', 'src'), 'rcv'), parts along dimension 1
The draws below stay inside these ranges and needn't reach their ends.
There are 2 independent parts, one for each index of `freq`. The reference program is written for one: setup_inputs(seed, part) draws one part's arguments, and reference() takes and returns one part's arrays. A program takes and returns all parts, laid end to end along the dimension named above; an argument that names none is the same for every part. Nothing has to cross between parts.
Inputs may be any that keep to these rules, and one draw needn't show every extreme that they name: A tile and its mirror tile are never both unrecorded; diagonal tiles are recorded.
All inputs are finite; a program needn't handle non-finite values.
Results may differ from the reference program's by a relative error of at most 0.0039.
Values may be sent and summed in bfloat16 or wider, within the bound.
No kernel may reach another device: no remote copies, remote signals or barrier semaphores. Data moves between devices by JAX's collectives and lax.ppermute only.
A program may use at most 192 MiB of HBM per device.

```python
import math
import jax
import jax.numpy as jnp
from jax import lax

N = 6144
PANEL = 768
LEVELS = 8
NT = 4
N_SRC = 4


def draw_unrecorded(key, part):
    key = jax.random.fold_in(key, 11)
    states = jax.random.randint(key, (NT, NT), 0, 3)
    rows_index = jnp.arange(NT)[:, None]
    cols_index = jnp.arange(NT)[None, :]
    upper = rows_index < cols_index
    lower = rows_index > cols_index
    first = jnp.where(upper & (states == 1), 1, 0)
    second = jnp.where(lower & (states.T == 2), 1, 0)
    return (first + second).astype(jnp.int32)


def touch_ends(entries, stream_key, low, largest):
    shape = entries.shape
    spot = [jax.random.randint(jax.random.fold_in(stream_key, axis), (), 0, shape[axis]) for axis in range(len(shape))]
    entries = entries.at[tuple(spot)].set(low)
    longest = shape.index(max(shape))
    spot[longest] = (spot[longest] + 1) % shape[longest]
    return entries.at[tuple(spot)].set(largest)


def level_of(rng, extent, split, low, high):
    loudness, own = 1.0, jax.random.fold_in(rng, 6)
    for dim, shards_of in split:
        draws = jnp.exp(jax.random.uniform(jax.random.fold_in(own, dim), (shards_of,), jnp.float32, low / len(split), high / len(split)))
        loudness = loudness * jnp.repeat(draws, extent[dim] // shards_of).reshape([-1 if axis == dim else 1 for axis in range(len(extent))])
    return loudness


def noise(stream_key, extent, spread, bound, split=(), held_as=jnp.bfloat16):
    array = spread * jax.random.normal(stream_key, extent, jnp.float32)
    if split:
        array = array * level_of(stream_key, extent, split, -0.22, 0.18)
    return jnp.clip(array, -bound, bound).astype(held_as)


def setup_inputs(seed: int = 0, part: int = 0) -> dict:
    key_of = jax.random.split(jax.random.key(seed), 6)
    part_splits = jax.random.split(jax.random.fold_in(key_of[5], part), 6)
    return {
        "wavefield": noise(part_splits[0], (2, N, N), 0.13, 2.0, ((1, 4), (2, 4))),
        "unrecorded": draw_unrecorded(jax.random.fold_in(jax.random.fold_in(key_of[5], part), 71), part),
        "obliquity": touch_ends(jax.random.randint(part_splits[2], (NT, NT), 0, LEVELS), jax.random.fold_in(part_splits[2], 1), 0, LEVELS - 1).astype(jnp.int32),
        "scale_table": jnp.clip(jnp.exp(jax.random.uniform(key_of[3], (LEVELS,), jnp.float32, math.log(0.4), math.log(2.5))), 0.4, 2.5),
        "panel_index": jax.random.randint(part_splits[4], (2,), 0, N // PANEL).astype(jnp.int32),
    }


def reference(wavefield, unrecorded, obliquity, scale_table, panel_index):
    tile_rows = N // N_SRC
    count_tiles = N_SRC
    flipped = jnp.swapaxes(wavefield, 1, 2)
    shaped = wavefield.reshape(2, count_tiles, tile_rows, count_tiles, tile_rows)
    mirror = flipped.reshape(2, count_tiles, tile_rows, count_tiles, tile_rows)
    factor = scale_table[obliquity][None, :, None, :, None]
    marks = (unrecorded == 1)[None, :, None, :, None]
    scaled = (factor * mirror.astype(jnp.float32)).astype(jnp.bfloat16)
    filled = jnp.where(marks, scaled, shaped).reshape(2, N, N)
    real_part = jnp.zeros((N, N), jnp.float32)
    imag_part = jnp.zeros((N, N), jnp.float32)
    for panel_slot in range(2):
        panel_start = panel_index[panel_slot].astype(jnp.int32) * PANEL
        left = lax.dynamic_slice_in_dim(filled, panel_start, PANEL, 2)
        right = lax.dynamic_slice_in_dim(filled, panel_start, PANEL, 1)
        real_part = real_part + jnp.dot(left[0], right[0], preferred_element_type=jnp.float32) - jnp.dot(left[1], right[1], preferred_element_type=jnp.float32)
        imag_part = imag_part + jnp.dot(left[0], right[1], preferred_element_type=jnp.float32) + jnp.dot(left[1], right[0], preferred_element_type=jnp.float32)
    prediction = jnp.stack([real_part, imag_part])
    return (filled.astype(jnp.float32) - prediction).astype(jnp.bfloat16)
```

```python
import functools

import jax
import jax.numpy as jnp
from jax import lax
from jax.experimental import pallas as pl
from jax.experimental.pallas import tpu as pltpu
from jax.sharding import PartitionSpec as P

PANEL = 768
GRID = ("src", "rcv")


def from_root(shard, axis, root):
    mine = lax.axis_index(axis) == root
    return lax.psum(jnp.where(mine, shard, jnp.zeros_like(shard)), axis)


def refill(recorded, mirror, marks, levels, scale_table):
    height = recorded.shape[1]
    width = recorded.shape[2]
    per_block = marks.shape[1]
    tile_cols = width // per_block
    level_ids = jnp.arange(scale_table.shape[0], dtype=jnp.int32)
    factor = jnp.sum(
        jnp.where(levels[0][:, None] == level_ids[None, :], scale_table[None, :], 0.0), axis=1
    )
    scaled = (
        factor[None, None, :, None]
        * mirror.reshape(2, height, per_block, tile_cols).astype(jnp.float32)
    ).astype(jnp.bfloat16)
    kept = jnp.where(
        marks[0][None, None, :, None] == 1,
        scaled,
        recorded.reshape(2, height, per_block, tile_cols),
    )
    return kept.reshape(2, height, width)


def plain_shards(wavefield, unrecorded, obliquity, scale_table, panel_index):
    src_count = lax.axis_size("src")
    rcv_count = lax.axis_size("rcv")
    tile_rows = wavefield.shape[1]
    block_cols = wavefield.shape[2]
    per_block = block_cols // tile_rows
    strip_rows = tile_rows // rcv_count
    sectioned = wavefield.reshape(1, 2, rcv_count, strip_rows, per_block, tile_rows)
    sectioned = lax.all_to_all(sectioned, "rcv", split_axis=2, concat_axis=0, tiled=True)
    sectioned = sectioned.reshape(rcv_count, 2, strip_rows, per_block, tile_rows)
    sectioned = jnp.transpose(sectioned, (1, 2, 0, 3, 4)).reshape(
        1, 2, strip_rows, src_count, tile_rows
    )
    sectioned = lax.all_to_all(sectioned, "src", split_axis=3, concat_axis=0, tiled=True)
    sectioned = sectioned.reshape(1, src_count, 2, strip_rows, tile_rows)
    sectioned = lax.all_to_all(sectioned, "rcv", split_axis=1, concat_axis=0, tiled=True)
    mirrored = jnp.transpose(sectioned, (2, 4, 1, 0, 3)).reshape(2, tile_rows, block_cols)
    filled = refill(wavefield, mirrored, unrecorded, obliquity, scale_table)
    piece_cols = min(PANEL, tile_rows)
    pieces = PANEL // piece_cols
    real_part = jnp.zeros((tile_rows, block_cols), jnp.float32)
    imag_part = jnp.zeros((tile_rows, block_cols), jnp.float32)
    for panel_slot in range(2):
        panel_start = panel_index[panel_slot] * PANEL
        for piece_slot in range(pieces):
            piece_start = panel_start + piece_slot * piece_cols
            left = lax.dynamic_slice_in_dim(filled, piece_start % block_cols, piece_cols, 2)
            left = from_root(left, "rcv", piece_start // block_cols)
            owner = piece_start // tile_rows
            offset = piece_start % tile_rows
            right = from_root(lax.dynamic_slice_in_dim(filled, offset, piece_cols, 1), "src", owner)
            real_part = (
                real_part
                + jnp.dot(left[0], right[0], preferred_element_type=jnp.float32)
                - jnp.dot(left[1], right[1], preferred_element_type=jnp.float32)
            )
            imag_part = (
                imag_part
                + jnp.dot(left[0], right[1], preferred_element_type=jnp.float32)
                + jnp.dot(left[1], right[0], preferred_element_type=jnp.float32)
            )
    prediction = jnp.stack([real_part, imag_part])
    return (filled.astype(jnp.float32) - prediction).astype(jnp.bfloat16)


def device_id(a, b, side):
    return a * side + b


def among(me, ids):
    hit = jnp.zeros((), jnp.bool_)
    for i in ids:
        hit = hit | (me == i)
    return hit


def fetch_mirror(tile, unrecorded, side):
    rows = tile.shape[1]
    steps = 2
    straight_rows = rows // 12 * 7
    sub = (rows - straight_rows) // steps
    block = side // 2
    me = device_id(lax.axis_index("src"), lax.axis_index("rcv"), side)

    def ident(a, b):
        return device_id(a, b, side)

    off = [(a, b) for a in range(side) for b in range(side) if a != b]
    far = [(a, b) for a, b in off if a // block != b // block]
    near = [(a, b) for a, b in off if a // block == b // block]
    turns = [[(a, b) for a, b in far if b % block == turn] for turn in range(block)]
    mine = unrecorded[0, 0] == 1
    flag = mine.astype(jnp.int32).reshape(1)
    theirs = lax.ppermute(flag, GRID, [(ident(a, b), ident(b, a)) for a, b in off])[0] == 1
    passing = [
        lax.ppermute(flag, GRID, [(ident(a, b), ident(a, a)) for a, b in turn])[0] == 1
        for turn in turns
    ]

    def owners(group):
        straight = [(ident(b, a), ident(a, b)) for a, b in group]
        active = (mine & among(me, [d for _, d in straight])) | (
            theirs & among(me, [s for s, _ in straight])
        )
        return straight, active

    def near_transfer(group):
        straight, active = owners(group)
        return active, lambda tile, held: lax.ppermute(tile, GRID, straight)

    def far_transfer(group, through):
        straight, active = owners(group)
        first = [(ident(b, a), ident(a, a)) for a, b in group]
        second = [(ident(a, a), ident(a, b)) for a, b in group]
        active = active | (through & among(me, [m for m, _ in second]))

        def run(tile, held):
            hops = [
                lax.ppermute(
                    tile[:, straight_rows + n * sub : straight_rows + (n + 1) * sub], GRID, first
                )
                for n in range(steps)
            ]
            top = lax.ppermute(tile[:, :straight_rows], GRID, straight)
            parts = [lax.ppermute(hop, GRID, second) for hop in hops]
            return jnp.concatenate([top, *parts], axis=1)

        return active, run

    def either(transfers, otherwise, held):
        active, runs = zip(*transfers)
        index = jnp.zeros((), jnp.int32)
        for n, on in enumerate(active):
            index = jnp.where(on, n + 1, index)
        return lax.switch(index, [otherwise, *runs], tile, held)

    ways = (False, True)
    transfers = [near_transfer([(a, b) for a, b in near if (a < b) == way]) for way in ways]
    transfers += [
        far_transfer([(a, b) for a, b in turns[0] if (a < b) == way], passing[0]) for way in ways
    ]
    held = either(transfers, lambda tile, held: jnp.zeros_like(tile), tile)
    transfers = [
        far_transfer([(a, b) for a, b in turns[1] if (a < b) == way], passing[1]) for way in ways
    ]
    held = either(transfers, lambda tile, held: held, held)
    return held, mine


def turn_kernel(factor_ref, held_ref, out_ref):
    turned = jnp.transpose(held_ref[0])
    out_ref[0] = (factor_ref[0] * turned.astype(jnp.float32)).astype(out_ref.dtype)


def turned_and_scaled(held, factor):
    rows, cols = held.shape[1:]
    size = 768
    return pl.pallas_call(
        turn_kernel,
        grid=(2, cols // size, rows // size),
        in_specs=[
            pl.BlockSpec(memory_space=pltpu.SMEM),
            pl.BlockSpec((1, size, size), lambda p, i, j: (p, j, i)),
        ],
        out_specs=pl.BlockSpec((1, size, size), lambda p, i, j: (p, i, j)),
        out_shape=jax.ShapeDtypeStruct((2, cols, rows), held.dtype),
        compiler_params=pltpu.CompilerParams(vmem_limit_bytes=32 * 1024 * 1024),
    )(factor.reshape(1), held)


def subtract_kernel(
    skip_ref, left0_ref, left1_ref, filled_ref, rows0, end0, rows1, end1, out_ref, panel0, panel1, sems
):
    depth, size = panel0.shape[1:]
    column = pl.ds(pl.multiple_of(pl.program_id(0) * size, size), size)

    @pl.when(pl.program_id(1) == 0)
    def _():
        for n, (rows, end, panel) in enumerate(((rows0, end0, panel0), (rows1, end1, panel1))):
            skip = skip_ref[n]

            @pl.when(skip >= 0)
            def _():
                start = pl.multiple_of(jnp.maximum(skip, 0) * 16, 16)
                pltpu.make_async_copy(
                    rows.at[:, pl.ds(start, depth), column], panel, sems.at[n]
                ).start()

            @pl.when(skip < 0)
            def _():
                pltpu.make_async_copy(end.at[:, :, column], panel, sems.at[n]).start()

        for n, (end, panel) in enumerate(((end0, panel0), (end1, panel1))):
            pltpu.make_async_copy(end.at[:, :, column], panel, sems.at[n]).wait()

    def dot(x, y):
        return jnp.dot(x, y, preferred_element_type=jnp.float32)

    real = dot(left0_ref[0], panel0[0]) - dot(left0_ref[1], panel0[1])
    real += dot(left1_ref[0], panel1[0]) - dot(left1_ref[1], panel1[1])
    out_ref[0] = (filled_ref[0].astype(jnp.float32) - real).astype(out_ref.dtype)
    imag = dot(left0_ref[0], panel0[1]) + dot(left0_ref[1], panel0[0])
    imag += dot(left1_ref[0], panel1[1]) + dot(left1_ref[1], panel1[0])
    out_ref[1] = (filled_ref[1].astype(jnp.float32) - imag).astype(out_ref.dtype)


def subtract_products(filled, lefts, rights):
    rows, cols = filled.shape[1:]
    depth = lefts[0].shape[2]
    size = 512
    left = pl.BlockSpec((2, size, depth), lambda j, i: (0, i, 0))
    block = pl.BlockSpec((2, size, size), lambda j, i: (0, i, j))
    whole = pl.BlockSpec(memory_space=pl.ANY)
    skips = jnp.stack([skip for _, skip, _ in rights])
    return pl.pallas_call(
        subtract_kernel,
        grid=(cols // size, rows // size),
        in_specs=[pl.BlockSpec(memory_space=pltpu.SMEM), left, left, block] + [whole] * 4,
        out_specs=block,
        out_shape=jax.ShapeDtypeStruct((2, rows, cols), filled.dtype),
        scratch_shapes=[
            pltpu.VMEM((2, depth, size), filled.dtype),
            pltpu.VMEM((2, depth, size), filled.dtype),
            pltpu.SemaphoreType.DMA((2,)),
        ],
        compiler_params=pltpu.CompilerParams(vmem_limit_bytes=48 * 1024 * 1024),
    )(skips, *lefts, filled, *[x for got, _, end in rights for x in (got, end)])


def spread(roots, side, count, owned):
    z = lax.axis_index("src")
    last = side - 1
    panels = range(len(roots))
    depth = owned[0].shape[1]
    height = depth // count
    reach = [max(root, last - root) for root in roots]
    way = [1 if last - root >= root else -1 for root in roots]
    current, received, end = [], [], []
    for q in panels:
        root, right = roots[q], owned[q]
        current.append(right[:, :height])
        received.append([])
        behind = root - way[q]
        end.append(
            lax.ppermute(right, "src", [(root, behind)]) if 0 <= behind <= last else right
        )
    for t in range(count + max(reach) - 1):
        for q in panels:
            if t >= count + reach[q] - 1:
                continue
            root, right = roots[q], owned[q]
            sent = current[q]
            back = t - 2 if q == 0 else t - 1
            other = received[1 - q]
            if back >= 0 and back < len(other):
                sent, _ = lax.optimization_barrier((sent, other[back]))
            links = [
                (root + way[q] * h, root + way[q] * (h + 1)) for h in range(reach[q]) if t - h < count
            ]
            got = lax.ppermute(sent, "src", links)
            received[q].append(got)
            if t + 1 < count:
                nxt = right[:, (t + 1) * height : (t + 2) * height]
                got = jnp.where(z == root, nxt, got)
            current[q] = got
    results = []
    for q in panels:
        root = roots[q]
        got = received[q] + [jnp.zeros_like(received[q][0])] * (count + last - 1 - len(received[q]))
        skip = (jnp.abs(z - root) - 1) * (height // 16)
        at_once = (z == root) | (z == root - way[q])
        results.append(
            (
                jnp.concatenate(got, axis=1),
                jnp.where(at_once, -1, skip),
                jnp.where(z == root, owned[q], end[q]),
            )
        )
    return results


def shards(wavefield, unrecorded, obliquity, scale_table, panel_index):
    side = lax.axis_size("src")
    tile_rows = wavefield.shape[1]
    tile_cols = wavefield.shape[2]
    if side != 4 or lax.axis_size("rcv") != 4 or tile_rows != tile_cols or tile_rows % PANEL:
        return plain_shards(wavefield, unrecorded, obliquity, scale_table, panel_index)
    per_tile = tile_rows // PANEL
    count = 8

    held, mine = fetch_mirror(wavefield, unrecorded, side)
    level_ids = jnp.arange(scale_table.shape[0], dtype=jnp.int32)
    factor = jnp.sum(jnp.where(obliquity[0, 0] == level_ids, scale_table, 0.0))
    filled = lax.cond(
        mine,
        lambda w, h, f: turned_and_scaled(h, f),
        lambda w, h, f: w,
        wavefield,
        held,
        factor,
    )
    lefts, owned = [], []
    for slot in range(2):
        offset = panel_index[slot] % per_tile * PANEL
        left = lax.dynamic_slice_in_dim(filled, offset, PANEL, 2)
        lefts.append(from_root(left, "rcv", panel_index[slot] // per_tile))
        owned.append(lax.dynamic_slice_in_dim(filled, offset, PANEL, 1))
    spreads = [
        functools.partial(spread, (first, second), side, count)
        for first in range(side)
        for second in range(side)
    ]
    which = panel_index[0] // per_tile * side + panel_index[1] // per_tile
    rights = lax.switch(which, spreads, owned)
    return subtract_products(filled, lefts, rights)


def solution(mesh):
    return jax.shard_map(
        shards,
        mesh=mesh,
        in_specs=(
            P(None, ("freq", "src"), "rcv"),
            P(("freq", "src"), "rcv"),
            P(("freq", "src"), "rcv"),
            P(),
            P("freq"),
        ),
        out_specs=P(None, ("freq", "src"), "rcv"),
        check_vma=False,
    )
```

```python
import functools

import jax
import jax.numpy as jnp
from jax import lax
from jax.experimental import pallas as pl
from jax.experimental.pallas import tpu as pltpu
from jax.sharding import PartitionSpec as P

PANEL = 768
GRID = ("src", "rcv")


def from_root(shard, axis, root):
    mine = lax.axis_index(axis) == root
    return lax.psum(jnp.where(mine, shard, jnp.zeros_like(shard)), axis)


def refill(recorded, mirror, marks, levels, scale_table):
    height = recorded.shape[1]
    width = recorded.shape[2]
    per_block = marks.shape[1]
    tile_cols = width // per_block
    level_ids = jnp.arange(scale_table.shape[0], dtype=jnp.int32)
    factor = jnp.sum(
        jnp.where(levels[0][:, None] == level_ids[None, :], scale_table[None, :], 0.0), axis=1
    )
    scaled = (
        factor[None, None, :, None]
        * mirror.reshape(2, height, per_block, tile_cols).astype(jnp.float32)
    ).astype(jnp.bfloat16)
    kept = jnp.where(
        marks[0][None, None, :, None] == 1,
        scaled,
        recorded.reshape(2, height, per_block, tile_cols),
    )
    return kept.reshape(2, height, width)


def plain_shards(wavefield, unrecorded, obliquity, scale_table, panel_index):
    src_count = lax.axis_size("src")
    rcv_count = lax.axis_size("rcv")
    tile_rows = wavefield.shape[1]
    block_cols = wavefield.shape[2]
    per_block = block_cols // tile_rows
    strip_rows = tile_rows // rcv_count
    sectioned = wavefield.reshape(1, 2, rcv_count, strip_rows, per_block, tile_rows)
    sectioned = lax.all_to_all(sectioned, "rcv", split_axis=2, concat_axis=0, tiled=True)
    sectioned = sectioned.reshape(rcv_count, 2, strip_rows, per_block, tile_rows)
    sectioned = jnp.transpose(sectioned, (1, 2, 0, 3, 4)).reshape(
        1, 2, strip_rows, src_count, tile_rows
    )
    sectioned = lax.all_to_all(sectioned, "src", split_axis=3, concat_axis=0, tiled=True)
    sectioned = sectioned.reshape(1, src_count, 2, strip_rows, tile_rows)
    sectioned = lax.all_to_all(sectioned, "rcv", split_axis=1, concat_axis=0, tiled=True)
    mirrored = jnp.transpose(sectioned, (2, 4, 1, 0, 3)).reshape(2, tile_rows, block_cols)
    filled = refill(wavefield, mirrored, unrecorded, obliquity, scale_table)
    piece_cols = min(PANEL, tile_rows)
    pieces = PANEL // piece_cols
    real_part = jnp.zeros((tile_rows, block_cols), jnp.float32)
    imag_part = jnp.zeros((tile_rows, block_cols), jnp.float32)
    for panel_slot in range(2):
        panel_start = panel_index[panel_slot] * PANEL
        for piece_slot in range(pieces):
            piece_start = panel_start + piece_slot * piece_cols
            left = lax.dynamic_slice_in_dim(filled, piece_start % block_cols, piece_cols, 2)
            left = from_root(left, "rcv", piece_start // block_cols)
            owner = piece_start // tile_rows
            offset = piece_start % tile_rows
            right = from_root(lax.dynamic_slice_in_dim(filled, offset, piece_cols, 1), "src", owner)
            real_part = (
                real_part
                + jnp.dot(left[0], right[0], preferred_element_type=jnp.float32)
                - jnp.dot(left[1], right[1], preferred_element_type=jnp.float32)
            )
            imag_part = (
                imag_part
                + jnp.dot(left[0], right[1], preferred_element_type=jnp.float32)
                + jnp.dot(left[1], right[0], preferred_element_type=jnp.float32)
            )
    prediction = jnp.stack([real_part, imag_part])
    return (filled.astype(jnp.float32) - prediction).astype(jnp.bfloat16)


def among(me, ids):
    hit = jnp.zeros((), jnp.bool_)
    for i in ids:
        hit = hit | (me == i)
    return hit


def fetch_mirror(tile, unrecorded, side):
    rows = tile.shape[1]
    steps = 4
    sub = rows // steps
    me = lax.axis_index("src") * side + lax.axis_index("rcv")

    def ident(a, b):
        return a * side + b

    off = [(a, b) for a in range(side) for b in range(side) if a != b]
    bent = [(a, b) for a, b in off if a + b == side - 1]
    mine = unrecorded[0, 0] == 1
    flag = mine.astype(jnp.int32).reshape(1)
    theirs = lax.ppermute(flag, GRID, [(ident(a, b), ident(b, a)) for a, b in off])[0] == 1
    passing = lax.ppermute(flag, GRID, [(ident(a, b), ident(a, a)) for a, b in bent])[0] == 1

    def owners(group):
        straight = [(ident(b, a), ident(a, b)) for a, b in group]
        active = (mine & among(me, [d for _, d in straight])) | (
            theirs & among(me, [s for s, _ in straight])
        )
        return straight, active

    def straight_transfer(group):
        straight, active = owners(group)
        return active, lambda tile: lax.ppermute(tile, GRID, straight)

    def bent_transfer(group):
        _, active = owners(group)
        first = [(ident(b, a), ident(a, a)) for a, b in group]
        second = [(ident(a, a), ident(a, b)) for a, b in group]
        active = active | (passing & among(me, [m for m, _ in second]))

        def run(tile):
            hops = [
                lax.ppermute(tile[:, n * sub : (n + 1) * sub], GRID, first) for n in range(steps)
            ]
            return jnp.concatenate([lax.ppermute(hop, GRID, second) for hop in hops], axis=1)

        return active, run

    transfers = []
    for way in (False, True):
        group = [(a, b) for a, b in off if (a < b) == way]
        transfers.append(straight_transfer([ab for ab in group if ab not in bent]))
        transfers.append(bent_transfer([ab for ab in group if ab in bent]))
    active, runs = zip(*transfers)
    index = jnp.zeros((), jnp.int32)
    for n, on in enumerate(active):
        index = jnp.where(on, n + 1, index)
    return lax.switch(index, [jnp.zeros_like, *runs], tile)


def fill_kernel(take_ref, factor_ref, tile_ref, held_ref, out_ref):
    @pl.when(take_ref[0] == 1)
    def _():
        turned = jnp.transpose(held_ref[0])
        out_ref[0] = (factor_ref[0] * turned.astype(jnp.float32)).astype(out_ref.dtype)

    @pl.when(take_ref[0] != 1)
    def _():
        out_ref[...] = tile_ref[...]


def fill(tile, held, take, factor):
    size = 768

    def kept(p, i, j, take, factor):
        keep = (take[0] != 1).astype(jnp.int32)
        return p * keep, i * keep, j * keep

    def mirrored(p, i, j, take, factor):
        turn = (take[0] == 1).astype(jnp.int32)
        return p * turn, j * turn, i * turn

    return pl.pallas_call(
        fill_kernel,
        grid_spec=pltpu.PrefetchScalarGridSpec(
            num_scalar_prefetch=2,
            grid=(2, tile.shape[1] // size, tile.shape[2] // size),
            in_specs=[pl.BlockSpec((1, size, size), kept), pl.BlockSpec((1, size, size), mirrored)],
            out_specs=pl.BlockSpec((1, size, size), lambda p, i, j, take, factor: (p, i, j)),
        ),
        out_shape=jax.ShapeDtypeStruct(tile.shape, tile.dtype),
        compiler_params=pltpu.CompilerParams(vmem_limit_bytes=40 * 1024 * 1024),
    )(take.reshape(1), factor.reshape(1), tile, held)


def subtract_kernel(
    skip_ref, left0_ref, left1_ref, filled_ref, rows0, end0, rows1, end1, out_ref, panel0, panel1, minus, sems
):
    depth = panel0.shape[1]

    @pl.when(pl.program_id(0) == 0)
    def _():
        for n, (rows, end, panel) in enumerate(((rows0, end0, panel0), (rows1, end1, panel1))):
            skip = skip_ref[n]

            @pl.when(skip >= 0)
            def _():
                start = pl.multiple_of(jnp.maximum(skip, 0) * 16, 16)
                pltpu.make_async_copy(rows.at[:, pl.ds(start, depth)], panel, sems.at[n]).start()

            @pl.when(skip < 0)
            def _():
                pltpu.make_async_copy(end, panel, sems.at[n]).start()

        for n, (end, panel) in enumerate(((end0, panel0), (end1, panel1))):
            pltpu.make_async_copy(end, panel, sems.at[n]).wait()
            minus[n] = -panel[1]

    left = jnp.concatenate([left0_ref[0], left0_ref[1], left1_ref[0], left1_ref[1]], axis=1)
    real = [panel0[0], minus[0], panel1[0], minus[1]]
    imag = [panel0[1], panel0[0], panel1[1], panel1[0]]
    for plane, right in enumerate((real, imag)):
        product = jnp.dot(
            left, jnp.concatenate(right, axis=0), preferred_element_type=jnp.float32
        )
        out_ref[plane] = (filled_ref[plane].astype(jnp.float32) - product).astype(out_ref.dtype)


def subtract_products(filled, lefts, rights):
    rows, cols = filled.shape[1:]
    depth = lefts[0].shape[2]
    size = 256
    left = pl.BlockSpec((2, size, depth), lambda i: (0, i, 0))
    block = pl.BlockSpec((2, size, cols), lambda i: (0, i, 0))
    whole = pl.BlockSpec(memory_space=pl.ANY)
    skips = jnp.stack([skip for _, skip, _ in rights])
    panel = pltpu.VMEM((2, depth, cols), filled.dtype)
    return pl.pallas_call(
        subtract_kernel,
        grid=(rows // size,),
        in_specs=[pl.BlockSpec(memory_space=pltpu.SMEM), left, left, block] + [whole] * 4,
        out_specs=block,
        out_shape=jax.ShapeDtypeStruct((2, rows, cols), filled.dtype),
        scratch_shapes=[panel, panel, panel, pltpu.SemaphoreType.DMA((2,))],
        compiler_params=pltpu.CompilerParams(vmem_limit_bytes=56 * 1024 * 1024),
    )(skips, *lefts, filled, *[x for got, _, end in rights for x in (got, end)])


def spread(roots, side, count, owned):
    z = lax.axis_index("src")
    last = side - 1
    panels = range(len(roots))
    depth = owned[0].shape[1]
    height = depth // count
    reach = [max(root, last - root) for root in roots]
    way = [1 if last - root >= root else -1 for root in roots]
    current, received, end = [], [], []
    for q in panels:
        root, right = roots[q], owned[q]
        current.append(right[:, :height])
        received.append([])
        behind = root - way[q]
        end.append(
            lax.ppermute(right, "src", [(root, behind)]) if 0 <= behind <= last else right
        )
    for t in range(count + max(reach) - 1):
        for q in panels:
            if t >= count + reach[q] - 1:
                continue
            root, right = roots[q], owned[q]
            sent = current[q]
            back = t - 2 if q == 0 else t - 1
            other = received[1 - q]
            if back >= 0 and back < len(other):
                sent, _ = lax.optimization_barrier((sent, other[back]))
            links = [
                (root + way[q] * h, root + way[q] * (h + 1)) for h in range(reach[q]) if t - h < count
            ]
            got = lax.ppermute(sent, "src", links)
            current[q] = got
            if t + 1 < count:
                nxt = right[:, (t + 1) * height : (t + 2) * height]
                current[q] = jnp.where(z == root, nxt, got)
            if t < count:
                got = jnp.where(z == root, right[:, t * height : (t + 1) * height], got)
            received[q].append(got)
    results = []
    for q in panels:
        root = roots[q]
        got = received[q] + [jnp.zeros_like(received[q][0])] * (count + last - 1 - len(received[q]))
        skip = jnp.maximum(jnp.abs(z - root) - 1, 0) * (height // 16)
        skip = jnp.where(z == root - way[q], -1, skip)
        results.append((jnp.concatenate(got, axis=1), skip, end[q]))
    return results


def shards(wavefield, unrecorded, obliquity, scale_table, panel_index):
    side = lax.axis_size("src")
    tile_rows = wavefield.shape[1]
    tile_cols = wavefield.shape[2]
    if side != 4 or lax.axis_size("rcv") != 4 or tile_rows != tile_cols or tile_rows % PANEL:
        return plain_shards(wavefield, unrecorded, obliquity, scale_table, panel_index)
    per_tile = tile_rows // PANEL
    count = 8

    level_ids = jnp.arange(scale_table.shape[0], dtype=jnp.int32)
    factor = jnp.sum(jnp.where(obliquity[0, 0] == level_ids, scale_table, 0.0))
    held = fetch_mirror(wavefield, unrecorded, side)
    filled = fill(wavefield, held, unrecorded[0, 0], factor)
    lefts, owned = [], []
    for slot in range(2):
        offset = panel_index[slot] % per_tile * PANEL
        left = lax.dynamic_slice_in_dim(filled, offset, PANEL, 2)
        lefts.append(from_root(left, "rcv", panel_index[slot] // per_tile))
        owned.append(lax.dynamic_slice_in_dim(filled, offset, PANEL, 1))
    spreads = [
        functools.partial(spread, (first, second), side, count)
        for first in range(side)
        for second in range(side)
    ]
    which = panel_index[0] // per_tile * side + panel_index[1] // per_tile
    rights = lax.switch(which, spreads, owned)
    return subtract_products(filled, lefts, rights)


def solution(mesh):
    return jax.shard_map(
        shards,
        mesh=mesh,
        in_specs=(
            P(None, ("freq", "src"), "rcv"),
            P(("freq", "src"), "rcv"),
            P(("freq", "src"), "rcv"),
            P(),
            P("freq"),
        ),
        out_specs=P(None, ("freq", "src"), "rcv"),
        check_vma=False,
    )
```

```python
import functools

import jax
import jax.numpy as jnp
from jax import lax
from jax.experimental import pallas as pl
from jax.experimental.pallas import tpu as pltpu
from jax.sharding import PartitionSpec as P

PANEL = 768
GRID = ("src", "rcv")


def from_root(shard, axis, root):
    mine = lax.axis_index(axis) == root
    return lax.psum(jnp.where(mine, shard, jnp.zeros_like(shard)), axis)


def refill(recorded, mirror, marks, levels, scale_table):
    height = recorded.shape[1]
    width = recorded.shape[2]
    per_block = marks.shape[1]
    tile_cols = width // per_block
    level_ids = jnp.arange(scale_table.shape[0], dtype=jnp.int32)
    factor = jnp.sum(
        jnp.where(levels[0][:, None] == level_ids[None, :], scale_table[None, :], 0.0), axis=1
    )
    scaled = (
        factor[None, None, :, None]
        * mirror.reshape(2, height, per_block, tile_cols).astype(jnp.float32)
    ).astype(jnp.bfloat16)
    kept = jnp.where(
        marks[0][None, None, :, None] == 1,
        scaled,
        recorded.reshape(2, height, per_block, tile_cols),
    )
    return kept.reshape(2, height, width)


def plain_shards(wavefield, unrecorded, obliquity, scale_table, panel_index):
    src_count = lax.axis_size("src")
    rcv_count = lax.axis_size("rcv")
    tile_rows = wavefield.shape[1]
    block_cols = wavefield.shape[2]
    per_block = block_cols // tile_rows
    strip_rows = tile_rows // rcv_count
    sectioned = wavefield.reshape(1, 2, rcv_count, strip_rows, per_block, tile_rows)
    sectioned = lax.all_to_all(sectioned, "rcv", split_axis=2, concat_axis=0, tiled=True)
    sectioned = sectioned.reshape(rcv_count, 2, strip_rows, per_block, tile_rows)
    sectioned = jnp.transpose(sectioned, (1, 2, 0, 3, 4)).reshape(
        1, 2, strip_rows, src_count, tile_rows
    )
    sectioned = lax.all_to_all(sectioned, "src", split_axis=3, concat_axis=0, tiled=True)
    sectioned = sectioned.reshape(1, src_count, 2, strip_rows, tile_rows)
    sectioned = lax.all_to_all(sectioned, "rcv", split_axis=1, concat_axis=0, tiled=True)
    mirrored = jnp.transpose(sectioned, (2, 4, 1, 0, 3)).reshape(2, tile_rows, block_cols)
    filled = refill(wavefield, mirrored, unrecorded, obliquity, scale_table)
    piece_cols = min(PANEL, tile_rows)
    pieces = PANEL // piece_cols
    real_part = jnp.zeros((tile_rows, block_cols), jnp.float32)
    imag_part = jnp.zeros((tile_rows, block_cols), jnp.float32)
    for panel_slot in range(2):
        panel_start = panel_index[panel_slot] * PANEL
        for piece_slot in range(pieces):
            piece_start = panel_start + piece_slot * piece_cols
            left = lax.dynamic_slice_in_dim(filled, piece_start % block_cols, piece_cols, 2)
            left = from_root(left, "rcv", piece_start // block_cols)
            owner = piece_start // tile_rows
            offset = piece_start % tile_rows
            right = from_root(lax.dynamic_slice_in_dim(filled, offset, piece_cols, 1), "src", owner)
            real_part = (
                real_part
                + jnp.dot(left[0], right[0], preferred_element_type=jnp.float32)
                - jnp.dot(left[1], right[1], preferred_element_type=jnp.float32)
            )
            imag_part = (
                imag_part
                + jnp.dot(left[0], right[1], preferred_element_type=jnp.float32)
                + jnp.dot(left[1], right[0], preferred_element_type=jnp.float32)
            )
    prediction = jnp.stack([real_part, imag_part])
    return (filled.astype(jnp.float32) - prediction).astype(jnp.bfloat16)


def among(me, ids):
    hit = jnp.zeros((), jnp.bool_)
    for i in ids:
        hit = hit | (me == i)
    return hit


def fetch_mirror(tile, unrecorded, side):
    rows = tile.shape[1]
    steps = 4
    sub = rows // steps
    me = lax.axis_index("src") * side + lax.axis_index("rcv")

    def ident(a, b):
        return a * side + b

    off = [(a, b) for a in range(side) for b in range(side) if a != b]
    bent = [(a, b) for a, b in off if a + b == side - 1]
    mine = unrecorded[0, 0] == 1
    flag = mine.astype(jnp.int32).reshape(1)
    theirs = lax.ppermute(flag, GRID, [(ident(a, b), ident(b, a)) for a, b in off])[0] == 1
    passing = lax.ppermute(flag, GRID, [(ident(a, b), ident(a, a)) for a, b in bent])[0] == 1

    def owners(group):
        straight = [(ident(b, a), ident(a, b)) for a, b in group]
        active = (mine & among(me, [d for _, d in straight])) | (
            theirs & among(me, [s for s, _ in straight])
        )
        return straight, active

    def straight_transfer(group):
        straight, active = owners(group)
        return active, lambda tile: lax.ppermute(tile, GRID, straight)

    def bent_transfer(group):
        _, active = owners(group)
        first = [(ident(b, a), ident(a, a)) for a, b in group]
        second = [(ident(a, a), ident(a, b)) for a, b in group]
        active = active | (passing & among(me, [m for m, _ in second]))

        def run(tile):
            hops = [
                lax.ppermute(tile[:, n * sub : (n + 1) * sub], GRID, first) for n in range(steps)
            ]
            return jnp.concatenate([lax.ppermute(hop, GRID, second) for hop in hops], axis=1)

        return active, run

    transfers = []
    for way in (False, True):
        group = [(a, b) for a, b in off if (a < b) == way]
        transfers.append(straight_transfer([ab for ab in group if ab not in bent]))
        transfers.append(bent_transfer([ab for ab in group if ab in bent]))
    active, runs = zip(*transfers)
    index = jnp.zeros((), jnp.int32)
    for n, on in enumerate(active):
        index = jnp.where(on, n + 1, index)
    return lax.switch(index, [jnp.zeros_like, *runs], tile)


def fill_kernel(take_ref, factor_ref, tile_ref, held_ref, out_ref):
    @pl.when(take_ref[0] == 1)
    def _():
        turned = jnp.transpose(held_ref[0])
        out_ref[0] = (factor_ref[0] * turned.astype(jnp.float32)).astype(out_ref.dtype)

    @pl.when(take_ref[0] != 1)
    def _():
        out_ref[...] = tile_ref[...]


def fill(tile, held, take, factor):
    size = 768

    def kept(p, i, j, take, factor):
        keep = (take[0] != 1).astype(jnp.int32)
        return p * keep, i * keep, j * keep

    def mirrored(p, i, j, take, factor):
        turn = (take[0] == 1).astype(jnp.int32)
        return p * turn, j * turn, i * turn

    return pl.pallas_call(
        fill_kernel,
        grid_spec=pltpu.PrefetchScalarGridSpec(
            num_scalar_prefetch=2,
            grid=(2, tile.shape[1] // size, tile.shape[2] // size),
            in_specs=[pl.BlockSpec((1, size, size), kept), pl.BlockSpec((1, size, size), mirrored)],
            out_specs=pl.BlockSpec((1, size, size), lambda p, i, j, take, factor: (p, i, j)),
        ),
        out_shape=jax.ShapeDtypeStruct(tile.shape, tile.dtype),
        compiler_params=pltpu.CompilerParams(vmem_limit_bytes=40 * 1024 * 1024),
    )(take.reshape(1), factor.reshape(1), tile, held)


def subtract_kernel(
    skip_ref, left0_ref, left1_ref, filled_ref, rows0, rows1, out_ref, panel0, panel1, minus, sems
):
    depth = panel0.shape[1]

    @pl.when(pl.program_id(0) == 0)
    def _():
        copies = []
        for n, (rows, panel) in enumerate(((rows0, panel0), (rows1, panel1))):
            start = pl.multiple_of(skip_ref[n] * 16, 16)
            copies.append(
                pltpu.make_async_copy(rows.at[:, pl.ds(start, depth)], panel, sems.at[n])
            )
            copies[n].start()
        for n, panel in enumerate((panel0, panel1)):
            copies[n].wait()
            minus[n] = -panel[1]

    left = jnp.concatenate([left0_ref[0], left0_ref[1], left1_ref[0], left1_ref[1]], axis=1)
    real = [panel0[0], minus[0], panel1[0], minus[1]]
    imag = [panel0[1], panel0[0], panel1[1], panel1[0]]
    for plane, right in enumerate((real, imag)):
        product = jnp.dot(
            left, jnp.concatenate(right, axis=0), preferred_element_type=jnp.float32
        )
        out_ref[plane] = (filled_ref[plane].astype(jnp.float32) - product).astype(out_ref.dtype)


def subtract_products(filled, lefts, rights):
    rows, cols = filled.shape[1:]
    depth = lefts[0].shape[2]
    size = 256
    left = pl.BlockSpec((2, size, depth), lambda i: (0, i, 0))
    block = pl.BlockSpec((2, size, cols), lambda i: (0, i, 0))
    whole = pl.BlockSpec(memory_space=pl.ANY)
    skips = jnp.stack([skip for _, skip in rights])
    panel = pltpu.VMEM((2, depth, cols), filled.dtype)
    return pl.pallas_call(
        subtract_kernel,
        grid=(rows // size,),
        in_specs=[pl.BlockSpec(memory_space=pltpu.SMEM), left, left, block] + [whole] * 2,
        out_specs=block,
        out_shape=jax.ShapeDtypeStruct((2, rows, cols), filled.dtype),
        scratch_shapes=[panel, panel, panel, pltpu.SemaphoreType.DMA((2,))],
        compiler_params=pltpu.CompilerParams(vmem_limit_bytes=56 * 1024 * 1024),
    )(skips, *lefts, filled, *[rows for rows, _ in rights])


def spread(roots, side, count, owned):
    z = lax.axis_index("src")
    last = side - 1
    panels = range(len(roots))
    depth = owned[0].shape[1]
    height = depth // count
    reach = [max(root, last - root) for root in roots]
    way = [1 if last - root >= root else -1 for root in roots]
    parts = count // 2
    current, received, direct = [], [], []
    for q in panels:
        current.append(owned[q][:, :height])
        received.append([])
        direct.append([None] * parts)

    def at_once(q, part):
        root, behind = roots[q], roots[q] - way[q]
        if not 0 <= behind <= last:
            return
        rows = owned[q][:, 2 * part * height : 2 * (part + 1) * height]
        if part:
            rows, _ = lax.optimization_barrier((rows, received[q][2 * part - 1]))
        direct[q][part] = lax.ppermute(rows, "src", [(root, behind)])

    for q in panels:
        at_once(q, 0)
    for t in range(count + max(reach) - 1):
        for q in panels:
            if t >= count + reach[q] - 1:
                continue
            root, right = roots[q], owned[q]
            sent = current[q]
            if t % 2 == 0 and 0 < t < count:
                if direct[q][t // 2 - 1] is not None:
                    sent, direct[q][t // 2 - 1] = lax.optimization_barrier(
                        (sent, direct[q][t // 2 - 1])
                    )
                at_once(q, t // 2)
            links = [
                (root + way[q] * h, root + way[q] * (h + 1)) for h in range(reach[q]) if t - h < count
            ]
            got = lax.ppermute(sent, "src", links)
            got, _ = lax.optimization_barrier((got, current[1 - q]))
            received[q].append(got)
            current[q] = got
            if t + 1 < count:
                nxt = right[:, (t + 1) * height : (t + 2) * height]
                current[q] = jnp.where(z == root, nxt, got)
    results = []
    for q in panels:
        root, right = roots[q], owned[q]
        rows = list(received[q])
        for t in range(count):
            if direct[q][t // 2] is not None:
                piece = direct[q][t // 2][:, t % 2 * height : (t % 2 + 1) * height]
                rows[t] = jnp.where(z == root - way[q], piece, rows[t])
            rows[t] = jnp.where(z == root, right[:, t * height : (t + 1) * height], rows[t])
        rows += [jnp.zeros_like(rows[0])] * (count + last - 1 - len(rows))
        skip = jnp.maximum(jnp.abs(z - root) - 1, 0) * (height // 16)
        results.append((jnp.concatenate(rows, axis=1), skip))
    return results


def shards(wavefield, unrecorded, obliquity, scale_table, panel_index):
    side = lax.axis_size("src")
    tile_rows = wavefield.shape[1]
    tile_cols = wavefield.shape[2]
    if side != 4 or lax.axis_size("rcv") != 4 or tile_rows != tile_cols or tile_rows % PANEL:
        return plain_shards(wavefield, unrecorded, obliquity, scale_table, panel_index)
    per_tile = tile_rows // PANEL
    count = 8

    level_ids = jnp.arange(scale_table.shape[0], dtype=jnp.int32)
    factor = jnp.sum(jnp.where(obliquity[0, 0] == level_ids, scale_table, 0.0))
    held = fetch_mirror(wavefield, unrecorded, side)
    filled = fill(wavefield, held, unrecorded[0, 0], factor)
    lefts, owned = [], []
    for slot in range(2):
        offset = panel_index[slot] % per_tile * PANEL
        left = lax.dynamic_slice_in_dim(filled, offset, PANEL, 2)
        lefts.append(from_root(left, "rcv", panel_index[slot] // per_tile))
        owned.append(lax.dynamic_slice_in_dim(filled, offset, PANEL, 1))
    spreads = [
        functools.partial(spread, (first, second), side, count)
        for first in range(side)
        for second in range(side)
    ]
    which = panel_index[0] // per_tile * side + panel_index[1] // per_tile
    rights = lax.switch(which, spreads, owned)
    return subtract_products(filled, lefts, rights)


def solution(mesh):
    return jax.shard_map(
        shards,
        mesh=mesh,
        in_specs=(
            P(None, ("freq", "src"), "rcv"),
            P(("freq", "src"), "rcv"),
            P(("freq", "src"), "rcv"),
            P(),
            P("freq"),
        ),
        out_specs=P(None, ("freq", "src"), "rcv"),
        check_vma=False,
    )
```
